256 devices in a mesh: seq: 32 (over x, y, core), head: 8 (over z).
Axes of the slice: x: 4, y: 4, z: 8, core: 2. Of those that a mesh axis runs over, the one named last changes fastest.
Arguments:
- queries: bfloat16 [2048, 64, 192], P('seq', 'head'), may hold values from -16 to 16
- span_latent: bfloat16 [2048, 576], P('seq'), may hold values from -4 to 4
- cache_latent: bfloat16 [2048, 576], P('seq'), may hold values from -4 to 4
- segments: int32 [2048], replicated, may hold values from 0 to 3, never falling along the last dimension, each value on 1 to 1024 neighbouring positions
- prefix_len: int32 [1], replicated, may hold values from 64 to 2048
- w_uk: bfloat16 [64, 128, 512], P('head'), may hold values from -0.25 to 0.25
- value_up_weight: bfloat16 [64, 512, 128], P('head'), may hold values from -0.5 to 0.5
- w_out: bfloat16 [8192, 7168], P('head', 'seq'), may hold values from -0.25 to 0.25
Outputs:
- attended: bfloat16 [2048, 7168], P('seq', 'head')
The draws below stay inside these ranges and needn't reach their ends.
All inputs are finite; a program needn't handle non-finite values.
Results may differ from the reference program's by a relative error of at most 0.014.
Values may be sent and summed in bfloat16 or wider, within the bound.
A program may use at most 128 MiB of HBM per device.

```python
import math
import jax
import jax.numpy as jnp
import numpy as np
from jax import lax

D = 7168
H = 64
KVL = 512
ROPE = 64
NOPE = 128
VD = 128
TOK_DEV = 64
SEGS = 4
SPAN = 2048


def draw_queries(key, part):
    key = jax.random.fold_in(key, 11)
    shape = (SPAN, H, NOPE + ROPE)
    values = jnp.clip(jax.random.normal(key, shape, jnp.float32), -6.0, 6.0)
    return values.astype(jnp.bfloat16)


def draw_span_latent(key, part):
    key = jax.random.fold_in(key, 23)
    shape = (SPAN, KVL + ROPE)
    values = jnp.clip(jax.random.normal(key, shape, jnp.float32), -4.0, 4.0)
    return values.astype(jnp.bfloat16)


def block_levels(key, extent, cuts, low, largest):
    def one(dim, parts):
        steps = jax.random.uniform(jax.random.fold_in(jax.random.fold_in(key, 6), dim), (parts,), jnp.float32, low / len(cuts), largest / len(cuts))
        return jnp.repeat(jnp.exp(steps), extent[dim] // parts).reshape((-1,) + (1,) * (len(extent) - dim - 1))

    level = one(*cuts[0])
    for cut in cuts[1:]:
        level = level * one(*cut)
    return level


def profile(count, total, most, skew):
    weights = [(1 << 20) // math.isqrt(rank ** skew) + 1 for rank in range(2, count + 1)]
    spare, holding = total - most - (count - 1), [1] * (count - 1)
    while spare > 0:
        free = [i for i in range(count - 1) if holding[i] < most]
        pool, budget = sum([weights[i] for i in free]), spare
        for i in free:
            more = min(most - holding[i], max(1, budget * weights[i] // pool), spare)
            holding[i] = holding[i] + more
            spare = spare - more
    return np.array([most] + holding)


def uneven_parts(stream_key, number_of, total, most, lean):
    if number_of == 2:
        one = jax.random.randint(stream_key, (), max(1, total - most), min(most, total - 1) + 1)
        return jnp.stack([one, total - one])
    tallies = jnp.asarray(profile(number_of, total, most, lean), jnp.int32)
    pairs = (number_of - 1) // 2
    giver, taker = tallies[1:1 + 2 * pairs:2], tallies[2:2 + 2 * pairs:2]
    room = jnp.minimum(giver - 1, most - taker)
    passed = jax.random.randint(jax.random.fold_in(stream_key, 1), (pairs,), 0, 1 << 20) % (room + 1)
    tallies = tallies.at[1:1 + 2 * pairs:2].set(giver - passed).at[2:2 + 2 * pairs:2].set(taker + passed)
    return tallies[jax.random.permutation(jax.random.fold_in(stream_key, 2), number_of)]


def noise(stream_key, extent, deviation, most, cuts=(), held_as=jnp.bfloat16):
    array = deviation * jax.random.normal(stream_key, extent, jnp.float32)
    if cuts:
        array = array * block_levels(stream_key, extent, cuts, -0.22, 0.18)
    return jnp.clip(array, -most, most).astype(held_as)


def setup_inputs(seed: int = 0) -> dict:
    keys = jax.random.split(jax.random.key(seed), 9)
    return {
        "queries": draw_queries(jax.random.fold_in(keys[8], 71), 0),
        "span_latent": draw_span_latent(jax.random.fold_in(keys[8], 71), 0),
        "cache_latent": noise(keys[2], (SPAN, KVL + ROPE), 1.0, 4.0, ((0, 32),)),
        "segments": jnp.searchsorted(jnp.cumsum(uneven_parts(keys[3], SEGS, SPAN, SPAN // 2, 2)), jnp.arange(SPAN), side="right").astype(jnp.int32),
        "prefix_len": jax.random.randint(keys[4], (1,), TOK_DEV, SPAN + 1).astype(jnp.int32),
        "w_uk": noise(keys[5], (H, NOPE, KVL), KVL ** -0.5, 0.25, ((0, 8),)),
        "value_up_weight": noise(keys[6], (H, KVL, VD), (KVL // 4) ** -0.5, 0.5, ((0, 8),)),
        "w_out": noise(keys[7], (H * VD, D), (H * VD // 16) ** -0.5, 0.25, ((0, 8), (1, 32))),
    }


def reference(queries, span_latent, cache_latent, segments, prefix_len, w_uk, value_up_weight, w_out):
    scaling = 1.0 / math.sqrt(NOPE + ROPE)
    query_latent = jnp.einsum('thn,hnk->thk', queries[:, :, :NOPE].astype(jnp.float32), w_uk.astype(jnp.float32)).astype(jnp.bfloat16)
    query_full = jnp.concatenate([query_latent, queries[:, :, NOPE:]], axis=2)
    key_rows = jnp.concatenate([cache_latent, span_latent], axis=0)
    position = jnp.arange(SPAN, dtype=jnp.int32)
    see_cache = (segments[:, None] == 0) & (position[None, :] < prefix_len[0])
    see_span = (segments[:, None] == segments[None, :]) & (position[None, :] <= position[:, None])
    visible = jnp.concatenate([see_cache, see_span], axis=1)

    def head_attention(query_rows):
        logit_scores = jnp.dot(query_rows, key_rows.T, preferred_element_type=jnp.float32) * scaling
        logit_scores = jnp.where(visible, logit_scores, jnp.float32(-1e+30))
        row_max = lax.optimization_barrier(jnp.max(logit_scores, axis=1, keepdims=True))
        expo = jnp.where(visible, jnp.exp(logit_scores - row_max), jnp.float32(0.0))
        row_total = lax.optimization_barrier(jnp.sum(expo, axis=1, keepdims=True))
        gathered_output = jnp.dot(expo.astype(jnp.bfloat16), key_rows[:, :KVL], preferred_element_type=jnp.float32)
        return (gathered_output / row_total).astype(jnp.bfloat16)
    blended_latent = lax.map(head_attention, jnp.swapaxes(query_full, 0, 1))
    head_split = jnp.einsum('bnw,bwd->nbd', blended_latent.astype(jnp.float32), value_up_weight.astype(jnp.float32)).astype(jnp.bfloat16)
    head_split = head_split.reshape(SPAN, H * VD)
    return jnp.dot(head_split, w_out, preferred_element_type=jnp.float32).astype(jnp.bfloat16)
```

```python
import functools
import math

import jax
import jax.numpy as jnp
from jax import lax
from jax.experimental import pallas as pl
from jax.experimental.pallas import tpu as pltpu
from jax.sharding import PartitionSpec as P

MESH = pl.DeviceIdType.MESH
F32 = jnp.float32
BF16 = jnp.bfloat16

SIDE = 4
CHIPS = 16
CORES = 2
DEPTH = 8
TOK = 64
HEADS = 8
NOPE = 128
ROPE = 64
LAT = 512
VD = 128
COLS = 224
ROWS = HEADS * CORES * TOK
TILE = 256
KEYS = SIDE * TOK
LOW = -1e30
MASKED = -2e30

A, B, WHOLE = (0, 32), (32, 32), (0, 64)
Q = [(0, 16), (16, 16), (32, 16), (48, 16)]


def _events():
    ev = [
        (0, 0, WHOLE, 0, 1),
        (0, 0, WHOLE, 0, 3),
        (0, 0, WHOLE, 1, 0),
        (0, 0, WHOLE, 3, 0),
        (0, 3, A, 0, 1),
        (0, 1, B, 0, 3),
        (3, 0, A, 1, 0),
        (1, 0, B, 3, 0),
    ]
    for dy in (3, 1, 2):
        ev += [(0, dy, A, 1, 0), (0, dy, A, 3, 0)]
    for dx in (3, 1, 2):
        ev += [(dx, 0, B, 0, 1), (dx, 0, B, 0, 3)]
    for dy in (3, 1, 2):
        ev += [(3, dy, Q[0], 1, 0), (1, dy, Q[1], 3, 0)]
    for dx in (3, 1, 2):
        ev += [(dx, 3, Q[2], 0, 1), (dx, 1, Q[3], 0, 3)]
    return ev


EVENTS = _events()


def kernel(
    q_ref, span_ref, cache_ref, seg_ref, pre_ref, wuk_hbm, vup_hbm, wo_hbm, out_ref,
    kv, qs, qf, m_ref, l_ref, acc, bias, wuk, vup, wo, pp, pr, pha, part, sp, rp, fs, fr,
    g1s, g1r, g2s, g2r, loc, sibs, sibr, rss, rsr, fss, fsr,
):
    s = lax.axis_index("seq")
    z = lax.axis_index("head")
    c = lax.rem(s, CORES)
    chip = s // CORES
    x = chip // SIDE
    y = lax.rem(chip, SIDE)

    def wrap(v, n):
        return lax.rem(v + n, n)

    def at(dx, dy):
        return wrap(x + dx, SIDE) * SIDE + wrap(y + dy, SIDE)

    def device(dx, dy):
        return (at(dx, dy) * CORES + c, z)

    sibling = (chip * CORES + 1 - c, z)
    up = (s, wrap(z + 1, DEPTH))
    down = (s, wrap(z + DEPTH - 1, DEPTH))

    target_head = 2 * x + y // 2

    def target(u):
        return ((wrap(x + u, SIDE) * SIDE + z // 2) * CORES + c, target_head)

    at_home = jnp.logical_and(y == z // 2, target_head == z)
    away = jnp.logical_not(at_home)

    barrier = pltpu.get_barrier_semaphore()
    near = [device(0, 1), device(0, 3), device(1, 0), device(3, 0), sibling, up, down]
    for dev in near:
        pl.semaphore_signal(barrier, inc=1, device_id=dev, device_id_type=MESH)
    home_x = z // 2
    home_y = 2 * lax.rem(z, 2)

    copies = [
        pltpu.make_async_copy(wuk_hbm, wuk, loc.at[0]),
        pltpu.make_async_copy(vup_hbm, vup, loc.at[1]),
        pltpu.make_async_copy(wo_hbm, wo.at[c], loc.at[2]),
    ]
    for cp in copies:
        cp.start()
    kv[chip, :, 0:LAT] = cache_ref[:, 0:LAT]
    kv[chip, :, LAT : 2 * LAT] = span_ref[:, 0:LAT]
    kv[chip, :, 2 * LAT : 2 * LAT + 2 * ROPE] = jnp.concatenate(
        [cache_ref[:, LAT:], span_ref[:, LAT:]], axis=1
    )

    pl.semaphore_wait(barrier, len(near))

    class Gather:
        def __init__(self, buf, send, recv):
            self.buf, self.send, self.recv = buf, send, recv

        def _copy(self, k, dx, dy, rows, sx, sy):
            ref = self.buf.at[at(dx, dy), pl.ds(rows[0], rows[1])]
            return pltpu.make_async_remote_copy(
                src_ref=ref, dst_ref=ref, send_sem=self.send.at[k], recv_sem=self.recv.at[k],
                device_id=device(sx, sy), device_id_type=MESH,
            )

        def start(self, *ks):
            for k in ks:
                self._copy(k, *EVENTS[k]).start()

        def wait(self, *ks):
            for k in ks:
                dx, dy, rows, sx, sy = EVENTS[k]
                self._copy(k, (dx - sx) % 4, (dy - sy) % 4, rows, sx, sy).wait_recv()

        def done(self):
            for k in range(len(EVENTS)):
                self._copy(k, *EVENTS[k]).wait_send()

        def run(self, on_line):
            self.start(0, 1, 2, 3)
            yield
            for got, sends in (
                (0, (4, 8, 9)), (1, (5, 10, 11)), (2, (6, 14, 15)), (3, (7, 16, 17)),
                (4, (12, 13)), (7, (18, 19)),
                (8, (20,)), (9, (21,)), (10, (22,)), (11, (23,)),
                (14, (26,)), (15, (27,)), (16, (28,)), (17, (29,)),
            ):
                self.wait(got)
                self.start(*sends)
            self.wait(5)
            on_line(0)
            for got, sends in ((12, (24,)), (13, (25,)), (18, (30,)), (19, (31,))):
                self.wait(got)
                self.start(*sends)
            self.wait(26, 27)
            on_line(3)
            self.wait(28, 29)
            on_line(1)
            self.wait(6, 20, 21, 22, 23, 24, 25, 30, 31)
            on_line(2)
            yield

    def to_sibling(src, dst, k):
        return pltpu.make_async_remote_copy(
            src_ref=src, dst_ref=dst, send_sem=sibs.at[k], recv_sem=sibr.at[k],
            device_id=sibling, device_id_type=MESH,
        )

    q_swap = to_sibling(q_ref, qs, 0)
    span_len = CHIPS * CORES * TOK
    token = (chip * (CORES * TOK) + lax.broadcasted_iota(jnp.int32, (CORES * TOK, 1), 0)).astype(F32)
    segs = seg_ref[...]
    firsts = [
        jnp.sum(jnp.sum((segs < k).astype(F32), axis=1, keepdims=True), axis=0, keepdims=True)
        for k in (1, 2, 3)
    ]
    start_of = jnp.zeros_like(token)
    for first in firsts:
        start_of = jnp.maximum(start_of, jnp.where(token >= first, first, 0.0))
    prefix = pre_ref[0].astype(F32)
    cache_end = jnp.where(token < firsts[0], prefix - 1.0, -1.0)
    exponent = math.log2(math.e) / math.sqrt(NOPE + ROPE)

    def attend(kind, dx):
        line = wrap(x + dx, SIDE)
        base = line * SIDE
        k_lat = kv[pl.ds(base, SIDE), :, kind * LAT : (kind + 1) * LAT].reshape(KEYS, LAT)
        k_rope = kv[pl.ds(base, SIDE), :, 2 * LAT : 2 * LAT + 2 * ROPE].reshape(KEYS, 2 * ROPE)
        lane = lax.broadcasted_iota(jnp.int32, (1, KEYS), 1)
        pos = (line * (SIDE * CORES * TOK) + (lane // TOK) * (CORES * TOK) + c * TOK + lax.rem(lane, TOK)).astype(F32)
        if kind == 0:
            seen = pos <= cache_end
        else:
            seen = jnp.logical_and(pos >= start_of, pos <= token)
        bias[...] = jnp.where(seen, 0.0, MASKED)

        def tile(i, carry):
            rows = pl.ds(pl.multiple_of(i * TILE, TILE), TILE)
            nt = (((1,), (1,)), ((), ()))
            sc = lax.dot_general(qf[rows, 0:LAT], k_lat, nt, preferred_element_type=F32)
            sc += lax.dot_general(
                qf[rows, LAT + kind * 2 * ROPE : LAT + (kind + 1) * 2 * ROPE], k_rope, nt,
                preferred_element_type=F32,
            )
            both = bias[...]
            sc = sc + jnp.concatenate([both, both], axis=0)
            m_old = m_ref[rows, :]
            m_new = jnp.maximum(m_old, jnp.max(sc, axis=1, keepdims=True))
            shrink = jnp.exp2((m_old - m_new) * exponent)
            p = jnp.exp2((sc - jnp.concatenate([m_new, m_new], axis=1)) * exponent)
            l_ref[rows, :] = l_ref[rows, :] * shrink + (p[:, 0:128] + p[:, 128:256])
            acc[rows, :] = acc[rows, :] * jnp.concatenate([shrink] * 4, axis=1) + jnp.dot(
                p.astype(BF16), k_lat, preferred_element_type=F32
            )
            m_ref[rows, :] = m_new
            return carry

        lax.fori_loop(0, ROWS // TILE, tile, 0, unroll=2)

    def keys_line(dx):
        if dx == 0:
            lift_queries()

        @pl.when(x < 2)
        def _():
            attend(0, dx)

        if dx == 0:
            attend(1, 0)
        elif dx == 3:

            @pl.when(x >= 1)
            def _():
                attend(1, 3)

        elif dx == 2:

            @pl.when(x >= 2)
            def _():
                attend(1, 2)

    def lift_queries():
        m_ref[...] = jnp.full_like(m_ref, LOW)
        l_ref[...] = jnp.zeros_like(l_ref)
        acc[...] = jnp.zeros_like(acc)
        copies[0].wait()
        row = lax.broadcasted_iota(jnp.int32, (HEADS * TOK, HEADS * TOK), 0)
        col = lax.broadcasted_iota(jnp.int32, (HEADS * TOK, HEADS * TOK), 1)
        order = (col == lax.rem(row, TOK) * HEADS + row // TOK).astype(BF16)
        nothing = jnp.zeros((TOK, ROPE), BF16)
        for src, core in ((q_ref, c), (qs, 1 - c)):
            if core is not c:
                q_swap.wait_recv()
            qp = jnp.dot(order, src[...], preferred_element_type=F32).astype(BF16)
            for h in range(HEADS):
                rows = pl.ds(pl.multiple_of(h * (CORES * TOK) + core * TOK, TOK), TOK)
                own = qp[h * TOK : (h + 1) * TOK]
                qf[rows, 0:LAT] = jnp.dot(own[:, 0:NOPE], wuk[h], preferred_element_type=F32).astype(BF16)
                qf[rows, LAT:] = jnp.concatenate([own[:, NOPE:], nothing, nothing, own[:, NOPE:]], axis=1)

    keys = Gather(kv, g1s, g1r)
    g = keys.run(keys_line)
    next(g)
    q_swap.start()
    wo_swap = to_sibling(wo_hbm, wo.at[c], 1)
    wo_swap.start()
    next(g)

    copies[1].wait()
    half = lax.broadcasted_iota(jnp.int32, (CORES * TOK, 128), 1) < 64
    swaps = []
    for t in range(4):
        for h in (2 * t, 2 * t + 1):
            rows = slice(h * CORES * TOK, (h + 1) * CORES * TOK)
            total = jnp.sum(l_ref[rows, :], axis=1, keepdims=True)
            o = (acc[rows, :] / jnp.where(total > 0.0, total, 1.0)).astype(BF16)
            ph = jnp.dot(o, vup[h], preferred_element_type=F32)
            pp[:, h, :, 0:VD] = ph.reshape(CORES, TOK, VD)
            pp[:, h, :, VD:] = jnp.where(half, m_ref[rows, :], total).reshape(CORES, TOK, 128)
        swap = to_sibling(pp.at[1 - c, pl.ds(2 * t, 2)], pr.at[pl.ds(2 * t, 2)], 2 + t)
        swap.start()
        swaps.append(swap)
    for t in range(4):
        swaps[t].wait_recv()
        for h in (2 * t, 2 * t + 1):
            own, other = pp[c, h], pr[h]
            m0, m1 = own[:, VD : VD + 1], other[:, VD : VD + 1]
            l0, l1 = own[:, VD + 64 : VD + 65], other[:, VD + 64 : VD + 65]
            top = jnp.maximum(m0, m1)
            w0 = l0 * jnp.exp2((m0 - top) * exponent)
            w1 = l1 * jnp.exp2((m1 - top) * exponent)
            norm = w0 + w1
            pha[chip, :, h * VD : (h + 1) * VD] = (
                own[:, 0:VD] * (w0 / norm) + other[:, 0:VD] * (w1 / norm)
            ).astype(BF16)

    copies[2].wait()
    to_sibling(wo_hbm, wo.at[1 - c], 1).wait_recv()

    def ring(u, k):
        forth = k < 4
        return pltpu.make_async_remote_copy(
            src_ref=sp.at[u, k], dst_ref=rp.at[u, k], send_sem=rss.at[u * 7 + k],
            recv_sem=rsr.at[u * 7 + k], device_id=up if forth else down, device_id_type=MESH,
        )

    def piece(u, j):
        return part[u, :, pl.ds(pl.multiple_of(j * 32, 32), 32), :]

    def step(u, k):
        for e, hop in ((k, z + 4 - k), (4 + k, z - 3 + k)):
            if e > 6:
                continue
            v = piece(u, wrap(hop + DEPTH, DEPTH))
            if k > 0:
                ring(u, e - 1).wait_recv()
                v = v + rp[u, e - 1].astype(F32)
            sp[u, e] = v.astype(BF16)
            ring(u, e).start()

    def home(u):
        return pltpu.make_async_remote_copy(
            src_ref=fs.at[u], dst_ref=fr.at[lax.rem(y, 2), lax.rem(z, 2)], send_sem=fss.at[u],
            recv_sem=fsr.at[lax.rem(y, 2) * 2 + lax.rem(z, 2)], device_id=target(u), device_id_type=MESH,
        )

    def finish(u):
        ring(u, 3).wait_recv()
        ring(u, 6).wait_recv()
        v = piece(u, z) + rp[u, 3].astype(F32) + rp[u, 6].astype(F32)
        fs[u] = v.astype(BF16)
        if u == 0:

            @pl.when(at_home)
            def _():
                fr[lax.rem(y, 2), lax.rem(z, 2)] = fs[u]

            @pl.when(away)
            def _():
                home(u).start()

        else:
            home(u).start()

    def out_line(dx):
        base = wrap(x + dx, SIDE) * SIDE
        rows = pha[pl.ds(base, SIDE)].reshape(SIDE * TOK, HEADS * VD)
        for i in range(CORES):
            part[dx, i] = jnp.dot(rows, wo[i], preferred_element_type=F32)
        step(dx, 0)
        if dx == 3:
            step(0, 1)
        if dx == 1:
            step(0, 2)
            step(3, 1)
        if dx == 2:
            step(0, 3)
            step(1, 1)
            step(3, 2)

    heads = Gather(pha, g2s, g2r)
    for _ in heads.run(out_line):
        pass
    finish(0)
    step(2, 1)
    step(1, 2)
    step(3, 3)
    finish(3)
    step(2, 2)
    step(1, 3)
    finish(1)
    step(2, 3)
    finish(2)

    for a in range(2):
        for b in range(2):
            mine = jnp.logical_and(
                jnp.logical_and(x == home_x, y == home_y + a), z == 2 * y + b
            )

            @pl.when(jnp.logical_not(mine))
            def _(a=a, b=b):
                pltpu.make_async_remote_copy(
                    src_ref=fs.at[0], dst_ref=fr.at[a, b], send_sem=fss.at[0],
                    recv_sem=fsr.at[a * 2 + b], device_id=sibling, device_id_type=MESH,
                ).wait_recv()

    for b in range(2):
        out_ref[b * 32 : (b + 1) * 32, :] = jnp.concatenate(
            [fr[a, b, i] for a in range(2) for i in range(CORES)], axis=1
        )

    keys.done()
    heads.done()
    q_swap.wait_send()
    wo_swap.wait_send()
    for t in range(4):
        swaps[t].wait_send()
    for u in range(4):
        for k in range(7):
            ring(u, k).wait_send()

    @pl.when(away)
    def _():
        home(0).wait_send()

    for u in range(1, 4):
        home(u).wait_send()


def on_device(queries, span_latent, cache_latent, segments, prefix_len, w_uk, value_up_weight, w_out):
    vmem = pl.BlockSpec(memory_space=pltpu.VMEM)
    smem = pl.BlockSpec(memory_space=pltpu.SMEM)
    hbm = pl.BlockSpec(memory_space=pl.ANY)
    dma = pltpu.SemaphoreType.DMA
    return pl.pallas_call(
        kernel,
        out_shape=jax.ShapeDtypeStruct((TOK, CORES * 2 * COLS), BF16),
        in_specs=[vmem, vmem, vmem, vmem, smem, hbm, hbm, hbm],
        out_specs=vmem,
        scratch_shapes=[
            pltpu.VMEM((CHIPS, TOK, 2 * LAT + 2 * ROPE), BF16),
            pltpu.VMEM((HEADS * TOK, NOPE + ROPE), BF16),
            pltpu.VMEM((ROWS, LAT + 4 * ROPE), BF16),
            pltpu.VMEM((ROWS, 128), F32),
            pltpu.VMEM((ROWS, 128), F32),
            pltpu.VMEM((ROWS, LAT), F32),
            pltpu.VMEM((CORES * TOK, KEYS), F32),
            pltpu.VMEM((HEADS, NOPE, LAT), BF16),
            pltpu.VMEM((HEADS, LAT, VD), BF16),
            pltpu.VMEM((CORES, HEADS * VD, COLS), BF16),
            pltpu.VMEM((CORES, HEADS, TOK, 2 * VD), F32),
            pltpu.VMEM((HEADS, TOK, 2 * VD), F32),
            pltpu.VMEM((CHIPS, TOK, HEADS * VD), BF16),
            pltpu.VMEM((4, CORES, SIDE * TOK, COLS), F32),
            pltpu.VMEM((4, 7, CORES, 32, COLS), BF16),
            pltpu.VMEM((4, 7, CORES, 32, COLS), BF16),
            pltpu.VMEM((4, CORES, 32, COLS), BF16),
            pltpu.VMEM((2, 2, CORES, 32, COLS), BF16),
            dma((32,)), dma((32,)), dma((32,)), dma((32,)),
            dma((3,)), dma((6,)), dma((6,)), dma((28,)), dma((28,)), dma((4,)), dma((4,)),
        ],
        compiler_params=pltpu.CompilerParams(
            collective_id=0, has_side_effects=True, vmem_limit_bytes=48 * 1024 * 1024
        ),
        name="prefill",
    )(
        queries.reshape(HEADS * TOK, NOPE + ROPE),
        span_latent,
        cache_latent,
        segments.reshape(CHIPS, CORES * TOK),
        prefix_len,
        w_uk,
        value_up_weight,
        w_out,
    )


def solution(mesh):
    placed = (
        P("seq", "head", None),
        P("seq", None),
        P("seq", None),
        P(),
        P(),
        P("head", None, None),
        P("head", None, None),
        P("head", "seq"),
    )
    return jax.shard_map(
        on_device, mesh=mesh, in_specs=placed, out_specs=P("seq", "head"), check_vma=False
    )
```

```python
import functools
import math

import jax
import jax.numpy as jnp
from jax import lax
from jax.experimental import pallas as pl
from jax.experimental.pallas import tpu as pltpu
from jax.sharding import PartitionSpec as P

MESH = pl.DeviceIdType.MESH
F32 = jnp.float32
BF16 = jnp.bfloat16

SIDE = 4
CHIPS = 16
CORES = 2
DEPTH = 8
TOK = 64
HEADS = 8
NOPE = 128
ROPE = 64
LAT = 512
VD = 128
COLS = 224
ROWS = HEADS * CORES * TOK
TILE = 512
KEYS = SIDE * TOK
LOW = -1e30
MASKED = -2e30

A, B, WHOLE = (0, 32), (32, 32), (0, 64)
Q = [(0, 16), (16, 16), (32, 16), (48, 16)]


def _by_neighbours():
    ev = [
        (0, 0, WHOLE, 0, 1),
        (0, 0, WHOLE, 0, 3),
        (0, 0, WHOLE, 1, 0),
        (0, 0, WHOLE, 3, 0),
        (0, 3, A, 0, 1),
        (0, 1, B, 0, 3),
        (3, 0, A, 1, 0),
        (1, 0, B, 3, 0),
    ]
    for dy in (3, 1, 2):
        ev += [(0, dy, A, 1, 0), (0, dy, A, 3, 0)]
    for dx in (3, 1, 2):
        ev += [(dx, 0, B, 0, 1), (dx, 0, B, 0, 3)]
    for dy in (3, 1, 2):
        ev += [(3, dy, Q[0], 1, 0), (1, dy, Q[1], 3, 0)]
    for dx in (3, 1, 2):
        ev += [(dx, 3, Q[2], 0, 1), (dx, 1, Q[3], 0, 3)]
    return ev


NEAR = _by_neighbours()
NEAR_1 = [(0, (4, 8, 9)), (1, (5, 10, 11)), (2, (6, 14, 15)), (3, (7, 16, 17))]
NEAR_2 = [
    (4, (12, 13)), (7, (18, 19)), (8, (20,)), (9, (21,)), (10, (22,)), (11, (23,)),
    (14, (26,)), (15, (27,)), (16, (28,)), (17, (29,)),
]
NEAR_3 = [(12, (24,)), (13, (25,)), (18, (30,)), (19, (31,))]


def _by_lines():
    ev = [(0, 0, WHOLE, 0, 1), (0, 0, WHOLE, 0, 3), (0, 0, WHOLE, 1, 0), (0, 0, WHOLE, 3, 0)]
    ev += [(0, 0, WHOLE, 0, 2), (0, 0, WHOLE, 2, 0)]
    ev += [(0, dy, A, sx, 0) for dy in (3, 1, 2) for sx in (1, 3, 2)]
    ev += [(dx, 0, B, 0, sy) for dx in (3, 1, 2) for sy in (1, 3, 2)]
    return ev


LINES = _by_lines()
LINES_1 = [
    (0, (6, 7, 8)), (1, (9, 10, 11)), (2, (15, 16, 17)), (3, (18, 19, 20)), (4, (12, 13, 14)), (5, (21, 22, 23)),
]


def kernel(
    q_hbm, span_hbm, cache_hbm, seg_hbm, pre_hbm, wuk_hbm, vup_hbm, wo_hbm, out_ref,
    q_ref, span_ref, cache_ref, seg_ref, pre_ref,
    kv, qs, qf, m_ref, l_ref, acc, bias, wuk, vup, wz, pp, pr, s1, r1, pha, s4, r4, r5,
    g1s, g1r, g2s, g2r, loc, sibs, sibr, wus, wur, wds, wdr, wps, wpr, s1s, s1r, s4s, s4r, s5s, s5r, known,
):
    s = lax.axis_index("seq")
    z = lax.axis_index("head")
    c = lax.rem(s, CORES)
    chip = s // CORES
    x = chip // SIDE
    y = lax.rem(chip, SIDE)

    def wrap(v, n):
        return lax.rem(v + n, n)

    def at(dx, dy):
        return wrap(x + dx, SIDE) * SIDE + wrap(y + dy, SIDE)

    def device(dx, dy):
        return (at(dx, dy) * CORES + c, z)

    sibling = (chip * CORES + 1 - c, z)
    up = (s, wrap(z + 1, DEPTH))
    down = (s, wrap(z + DEPTH - 1, DEPTH))

    copies = [
        pltpu.make_async_copy(src, dst, loc.at[i])
        for i, (src, dst) in enumerate(
            (
                (cache_hbm, cache_ref), (span_hbm, span_ref), (q_hbm, q_ref), (wuk_hbm, wuk),
                (seg_hbm, seg_ref), (pre_hbm, pre_ref), (vup_hbm, vup), (wo_hbm, wz.at[z, c]),
            )
        )
    ]
    for cp in copies:
        cp.start()

    barrier = pltpu.get_barrier_semaphore()
    near = [device(*d) for d in ((0, 1), (0, 3), (1, 0), (3, 0))] + [sibling, up, down]
    for dev in near:
        pl.semaphore_signal(barrier, inc=1, device_id=dev, device_id_type=MESH)

    copies[0].wait()
    copies[1].wait()
    kv[chip, :, 0:LAT] = cache_ref[:, 0:LAT]
    kv[chip, :, LAT : 2 * LAT] = span_ref[:, 0:LAT]
    kv[chip, :, 2 * LAT : 2 * LAT + 2 * ROPE] = jnp.concatenate(
        [cache_ref[:, LAT:], span_ref[:, LAT:]], axis=1
    )
    copies[2].wait()
    pl.semaphore_wait(barrier, len(near))

    def tell(n):
        for dev in (up, down):
            pl.semaphore_signal(known.at[n], inc=1, device_id=dev, device_id_type=MESH)

    def hear(n):
        pl.semaphore_wait(known.at[n], 2)

    tell(0)

    class Gather:
        def __init__(self, buf, send, recv, events, lanes):
            self.buf, self.send, self.recv, self.events, self.lanes = buf, send, recv, events, lanes

        def _copy(self, g, k, dx, dy, rows, sx, sy):
            ref = self.buf.at[at(dx, dy), pl.ds(*rows), pl.ds(*self.lanes[g])]
            n = g * len(self.events) + k
            return pltpu.make_async_remote_copy(
                src_ref=ref, dst_ref=ref, send_sem=self.send.at[n], recv_sem=self.recv.at[n],
                device_id=device(sx, sy), device_id_type=MESH,
            )

        def start(self, g, *ks):
            for k in ks:
                self._copy(g, k, *self.events[k]).start()

        def wait(self, g, *ks):
            for k in ks:
                dx, dy, rows, sx, sy = self.events[k]
                self._copy(g, k, (dx - sx) % 4, (dy - sy) % 4, rows, sx, sy).wait_recv()

        def follow(self, g, steps):
            for got, sends in steps:
                self.wait(g, got)
                self.start(g, *sends)

        def done(self):
            for g in range(len(self.lanes)):
                for k in range(len(self.events)):
                    self._copy(g, k, *self.events[k]).wait_send()

    def to_sibling(src, dst, k):
        return pltpu.make_async_remote_copy(
            src_ref=src, dst_ref=dst, send_sem=sibs.at[k], recv_sem=sibr.at[k],
            device_id=sibling, device_id_type=MESH,
        )

    keys = Gather(kv, g1s, g1r, NEAR, [(0, 2 * LAT + 2 * ROPE)])
    keys.start(0, 0, 1, 2, 3)
    q_swap = to_sibling(q_ref, qs, 0)
    q_swap.start()

    def around(way, i):
        half = i % 2 if i < 6 or way > 0 else 1
        block = wrap(z - way * (i // 2) + DEPTH, DEPTH)
        ref = wz.at[block, c, pl.ds(half * (COLS // 2), COLS // 2)]
        send, recv = (wus, wur) if way > 0 else (wds, wdr)
        return pltpu.make_async_remote_copy(
            src_ref=ref, dst_ref=ref, send_sem=send.at[i], recv_sem=recv.at[i],
            device_id=up if way > 0 else down, device_id_type=MESH,
        )

    def around_landed(way, i):
        half = i % 2 if i < 6 or way > 0 else 1
        block = wrap(z - way * (i // 2 + 1) + DEPTH, DEPTH)
        ref = wz.at[block, c, pl.ds(half * (COLS // 2), COLS // 2)]
        send, recv = (wus, wur) if way > 0 else (wds, wdr)
        pltpu.make_async_remote_copy(
            src_ref=ref, dst_ref=ref, send_sem=send.at[i], recv_sem=recv.at[i],
            device_id=up if way > 0 else down, device_id_type=MESH,
        ).wait_recv()

    def pass_block(d, core):
        ref = wz.at[wrap(z + d + DEPTH, DEPTH), core]
        return pltpu.make_async_remote_copy(
            src_ref=ref, dst_ref=ref, send_sem=wps.at[d % DEPTH], recv_sem=wpr.at[d % DEPTH],
            device_id=sibling, device_id_type=MESH,
        )

    def weights_step(i):
        for way in (1, -1):
            around_landed(way, i)
            if i < 4:
                around(way, i + 2).start()
        if i == 4:
            around(1, 6).start()
        elif i == 5:
            around(-1, 6).start()
        if i % 2 == 1:
            pass_block(i // 2 + 1, c).start()
            pass_block(-(i // 2 + 1), c).start()
        elif i == 6:
            pass_block(4, c).start()

    copies[7].wait()
    for i in range(2):
        around(1, i).start()
        around(-1, i).start()
    pass_block(0, c).start()

    m_ref[...] = jnp.full_like(m_ref, LOW)
    l_ref[...] = jnp.zeros_like(l_ref)
    acc[...] = jnp.zeros_like(acc)
    row = lax.broadcasted_iota(jnp.int32, (HEADS * TOK, HEADS * TOK), 0)
    col = lax.broadcasted_iota(jnp.int32, (HEADS * TOK, HEADS * TOK), 1)
    by_head = (col == lax.rem(row, TOK) * HEADS + row // TOK).astype(BF16)
    copies[3].wait()
    for src, core in ((q_ref, c), (qs, 1 - c)):
        if src is qs:
            q_swap.wait_recv()
        qp = jnp.dot(by_head, src[...], preferred_element_type=F32).astype(BF16)
        for h in range(HEADS):
            rows = pl.ds(pl.multiple_of(h * (CORES * TOK) + core * TOK, TOK), TOK)
            own = qp[h * TOK : (h + 1) * TOK]
            qf[rows, 0:LAT] = jnp.dot(own[:, 0:NOPE], wuk[h], preferred_element_type=F32).astype(BF16)
            qf[rows, LAT:] = jnp.concatenate([own[:, NOPE:], own[:, NOPE:]], axis=1)

    copies[4].wait()
    copies[5].wait()
    token = (chip * (CORES * TOK) + lax.broadcasted_iota(jnp.int32, (CORES * TOK, 1), 0)).astype(F32)
    segs = seg_ref[...]
    firsts = [
        jnp.sum(jnp.sum((segs < k).astype(F32), axis=1, keepdims=True), axis=0, keepdims=True)
        for k in (1, 2, 3)
    ]
    start_of = jnp.zeros_like(token)
    for first in firsts:
        start_of = jnp.maximum(start_of, jnp.where(token >= first, first, 0.0))
    prefix = pre_ref[0].astype(F32)
    cache_end = jnp.where(token < firsts[0], prefix - 1.0, -1.0)
    exponent = math.log2(math.e) / math.sqrt(NOPE + ROPE)

    def attend(*parts):
        latent, ropes, seen = [], [], []
        for kind, dx in parts:
            line = wrap(x + dx, SIDE)
            block = kv[pl.ds(line * SIDE, SIDE)].reshape(KEYS, 2 * LAT + 2 * ROPE)
            latent.append(block[:, kind * LAT : (kind + 1) * LAT])
            lane = lax.broadcasted_iota(jnp.int32, (KEYS, 2 * ROPE), 1)
            mine = lane < ROPE if kind == 0 else lane >= ROPE
            ropes.append(jnp.where(mine, block[:, 2 * LAT :], jnp.zeros((), BF16)))
            lane = lax.broadcasted_iota(jnp.int32, (1, KEYS), 1)
            pos = (
                line * (SIDE * CORES * TOK) + (lane // TOK) * (CORES * TOK) + c * TOK + lax.rem(lane, TOK)
            ).astype(F32)
            if kind == 0:
                seen.append(pos <= cache_end)
            else:
                seen.append(jnp.logical_and(pos >= start_of, pos <= token))
        values = jnp.concatenate(latent, axis=0)
        rows_k = jnp.concatenate([values, jnp.concatenate(ropes, axis=0)], axis=1)
        for i, ok in enumerate(seen):
            bias[:, i * KEYS : (i + 1) * KEYS] = jnp.where(ok, 0.0, MASKED)
        for i in range(ROWS // TILE):
            rows = slice(i * TILE, (i + 1) * TILE)
            sc = lax.dot_general(
                qf[rows, :], rows_k, (((1,), (1,)), ((), ())), preferred_element_type=F32
            )
            both = bias[...]
            sc = sc + jnp.concatenate([both] * (TILE // (CORES * TOK)), axis=0)
            m_old = m_ref[rows, :]
            m_new = jnp.maximum(m_old, jnp.max(sc, axis=1, keepdims=True))
            shrink = jnp.exp2((m_old - m_new) * exponent)
            p = jnp.exp2((sc - jnp.concatenate([m_new] * 4, axis=1)) * exponent)
            l_ref[rows, :] = l_ref[rows, :] * shrink + (
                (p[:, 0:128] + p[:, 128:256]) + (p[:, 256:384] + p[:, 384:512])
            )
            acc[rows, :] = acc[rows, :] * jnp.concatenate([shrink] * 4, axis=1) + jnp.dot(
                p.astype(BF16), values, preferred_element_type=F32
            )
            m_ref[rows, :] = m_new

    early = x < 2
    late = jnp.logical_not(early)

    keys.follow(0, NEAR_1)
    hear(0)
    tell(1)
    weights_step(0)
    keys.follow(0, NEAR_2)
    weights_step(1)
    keys.wait(0, 5)

    @pl.when(early)
    def _():
        attend((0, 0), (1, 0))

    hear(1)
    tell(2)
    keys.follow(0, NEAR_3)
    weights_step(2)
    keys.wait(0, 26, 27, 28, 29)

    @pl.when(early)
    def _():
        attend((0, 3), (0, 1))

    @pl.when(late)
    def _():
        attend((1, 0), (1, 3))

    keys.wait(0, 6, 20, 21, 22, 23, 24, 25, 30, 31)

    @pl.when(early)
    def _():
        attend((0, 2), (1, 3))

    @pl.when(late)
    def _():
        attend((1, 2), (1, 1))

    weights_step(3)
    hear(2)

    copies[6].wait()
    half = lax.broadcasted_iota(jnp.int32, (CORES * TOK, 128), 1) < 64
    swaps = []
    for t in range(4):
        for h in (2 * t, 2 * t + 1):
            rows = slice(h * CORES * TOK, (h + 1) * CORES * TOK)
            total = jnp.sum(l_ref[rows, :], axis=1, keepdims=True)
            o = (acc[rows, :] / jnp.where(total > 0.0, total, 1.0)).astype(BF16)
            ph = jnp.dot(o, vup[h], preferred_element_type=F32)
            pp[:, h, :, 0:VD] = ph.reshape(CORES, TOK, VD)
            pp[:, h, :, VD:] = jnp.where(half, m_ref[rows, :], total).reshape(CORES, TOK, 128)
        swap = to_sibling(pp.at[1 - c, pl.ds(2 * t, 2)], pr.at[pl.ds(2 * t, 2)], 2 + t)
        swap.start()
        swaps.append(swap)
    def dealt(g, d):
        to = wrap(z + d, DEPTH)
        return pltpu.make_async_remote_copy(
            src_ref=s1.at[g, to], dst_ref=r1.at[g, z], send_sem=s1s.at[g * DEPTH + d], recv_sem=s1r.at[g * DEPTH + z],
            device_id=(s, to), device_id_type=MESH,
        )

    def landed(src, dst, sem):
        pltpu.make_async_remote_copy(
            src_ref=src, dst_ref=dst, send_sem=s1s.at[0], recv_sem=sem, device_id=up, device_id_type=MESH
        ).wait_recv()

    far_first = (4, 3, 5, 2, 6, 1, 7)
    wide = HEADS * VD // 2
    for g in range(2):
        merged = []
        for t in (2 * g, 2 * g + 1):
            swaps[t].wait_recv()
            for h in (2 * t, 2 * t + 1):
                own, other = pp[c, h], pr[h]
                m0, m1 = own[:, VD : VD + 1], other[:, VD : VD + 1]
                l0, l1 = own[:, VD + 64 : VD + 65], other[:, VD + 64 : VD + 65]
                top = jnp.maximum(m0, m1)
                w0 = l0 * jnp.exp2((m0 - top) * exponent)
                w1 = l1 * jnp.exp2((m1 - top) * exponent)
                norm = w0 + w1
                merged.append(own[:, 0:VD] * (w0 / norm) + other[:, 0:VD] * (w1 / norm))
        left = jnp.concatenate(merged[:2], axis=1)
        right = jnp.concatenate(merged[2:], axis=1)
        for p in range(DEPTH):
            rows = slice(8 * p, 8 * p + 8)
            s1[g, p] = jnp.concatenate([left[rows], right[rows]], axis=0).astype(BF16)
        for d in far_first:
            dealt(g, d).start()
        r1[g, z] = s1[g, z]
    weights_step(4)

    heads = Gather(pha, g2s, g2r, LINES, [(0, wide), (wide, wide)])
    for g in range(2):
        for d in reversed(far_first):
            plane = wrap(z + d, DEPTH)
            landed(s1.at[0, 0], r1.at[g, plane], s1r.at[g * DEPTH + plane])
        blocks = []
        for p in range(DEPTH):
            rows = r1[g, p].astype(F32)
            blocks.append(jnp.concatenate([rows[0:8], rows[8:16]], axis=1))
        pha[chip, :, g * wide : (g + 1) * wide] = jnp.concatenate(blocks, axis=0).astype(BF16)
        heads.start(g, 4, 5, 0, 1, 2, 3)
    weights_step(5)
    for g in range(2):
        heads.follow(g, LINES_1)
    weights_step(6)
    for d in range(DEPTH):
        pass_block(d, 1 - c).wait_recv()

    even = lax.rem(lax.broadcasted_iota(jnp.int32, (COLS, CHIPS * 16), 1), 16) < 8
    sums = [[None, None], [None, None]]
    for g in range(2):
        heads.wait(g, *range(6, 24))
        lanes = slice(g * wide, (g + 1) * wide)
        for i in range(CORES):
            for parity in range(2):
                total = sums[i][parity]
                for p in range(DEPTH // 2):
                    rows = pha[:, 16 * p : 16 * p + 16, lanes].reshape(CHIPS * 16, wide)
                    v = lax.dot_general(
                        wz[2 * p + parity, i, :, lanes], rows, (((1,), (1,)), ((), ())),
                        preferred_element_type=F32,
                    )
                    total = v if total is None else total + v
                sums[i][parity] = total
    products = [jnp.where(even, *pair).T for pair in sums]
    for g in range(CHIPS):
        s4[g] = jnp.concatenate(
            [v[16 * g : 16 * g + 8] + v[16 * g + 8 : 16 * g + 16] for v in products], axis=0
        ).astype(BF16)

    others = [(dx, dy) for dx in (2, 1, 3, 0) for dy in (2, 1, 3, 0)][:-1]

    def over(dx, dy):
        return pltpu.make_async_remote_copy(
            src_ref=s4.at[at(dx, dy)], dst_ref=r4.at[chip], send_sem=s4s.at[dx * SIDE + dy], recv_sem=s4r.at[chip],
            device_id=device(dx, dy), device_id_type=MESH,
        )

    def along(d):
        plane = wrap(z + d, DEPTH)
        return pltpu.make_async_remote_copy(
            src_ref=r4.at[pl.ds(2 * plane, 2)], dst_ref=r5.at[z], send_sem=s5s.at[d], recv_sem=s5r.at[z],
            device_id=(s, plane), device_id_type=MESH,
        )

    for dx, dy in others:
        over(dx, dy).start()
    r4[chip] = s4[chip]
    for dx, dy in reversed(others):
        landed(s4.at[0], r4.at[at(dx, dy)], s4r.at[at(dx, dy)])
    for d in far_first:
        along(d).start()
    r5[z] = r4[pl.ds(2 * z, 2)]
    for d in reversed(far_first):
        plane = wrap(z + d, DEPTH)
        landed(r4.at[pl.ds(0, 2)], r5.at[plane], s5r.at[plane])
    columns = []
    for a in range(2):
        for i in range(CORES):
            columns.append(
                jnp.concatenate([r5[p, a].astype(F32)[8 * i : 8 * i + 8] for p in range(DEPTH)], axis=0)
            )
    out_ref[...] = jnp.concatenate(columns, axis=1).astype(BF16)

    keys.done()
    heads.done()
    q_swap.wait_send()
    for i in range(7):
        around(1, i).wait_send()
        around(-1, i).wait_send()
    for d in range(DEPTH):
        pass_block(d, c).wait_send()
    for d in far_first:
        dealt(0, d).wait_send()
        dealt(1, d).wait_send()
        along(d).wait_send()
    for dx, dy in others:
        over(dx, dy).wait_send()
    for t in range(4):
        swaps[t].wait_send()


def on_device(queries, span_latent, cache_latent, segments, prefix_len, w_uk, value_up_weight, w_out):
    hbm = pl.BlockSpec(memory_space=pltpu.HBM)
    dma = pltpu.SemaphoreType.DMA
    return pl.pallas_call(
        kernel,
        out_shape=jax.ShapeDtypeStruct((TOK, CORES * 2 * COLS), BF16),
        in_specs=[hbm] * 8,
        out_specs=pl.BlockSpec(memory_space=pltpu.VMEM),
        scratch_shapes=[
            pltpu.VMEM((HEADS * TOK, NOPE + ROPE), BF16),
            pltpu.VMEM((TOK, LAT + ROPE), BF16),
            pltpu.VMEM((TOK, LAT + ROPE), BF16),
            pltpu.VMEM((CHIPS, CORES * TOK), jnp.int32),
            pltpu.SMEM((1,), jnp.int32),
            pltpu.VMEM((CHIPS, TOK, 2 * LAT + 2 * ROPE), BF16),
            pltpu.VMEM((HEADS * TOK, NOPE + ROPE), BF16),
            pltpu.VMEM((ROWS, LAT + 2 * ROPE), BF16),
            pltpu.VMEM((ROWS, 128), F32),
            pltpu.VMEM((ROWS, 128), F32),
            pltpu.VMEM((ROWS, LAT), F32),
            pltpu.VMEM((CORES * TOK, 2 * KEYS), F32),
            pltpu.VMEM((HEADS, NOPE, LAT), BF16),
            pltpu.VMEM((HEADS, LAT, VD), BF16),
            pltpu.VMEM((DEPTH, CORES, COLS, HEADS * VD), BF16),
            pltpu.VMEM((CORES, HEADS, TOK, 2 * VD), F32),
            pltpu.VMEM((HEADS, TOK, 2 * VD), F32),
            pltpu.VMEM((2, DEPTH, 16, HEADS * VD // 4), BF16),
            pltpu.VMEM((2, DEPTH, 16, HEADS * VD // 4), BF16),
            pltpu.VMEM((CHIPS, TOK, HEADS * VD), BF16),
            pltpu.VMEM((CHIPS, 16, COLS), BF16),
            pltpu.VMEM((CHIPS, 16, COLS), BF16),
            pltpu.VMEM((DEPTH, 2, 16, COLS), BF16),
            dma((32,)), dma((32,)), dma((48,)), dma((48,)),
            dma((8,)), dma((6,)), dma((6,)), dma((7,)), dma((7,)), dma((7,)), dma((7,)), dma((8,)), dma((8,)),
            dma((16,)), dma((16,)), dma((16,)), dma((16,)), dma((8,)), dma((8,)),
            pltpu.SemaphoreType.REGULAR((3,)),
        ],
        compiler_params=pltpu.CompilerParams(
            collective_id=0, has_side_effects=True, vmem_limit_bytes=56 * 1024 * 1024
        ),
        name="prefill",
    )(
        queries.reshape(HEADS * TOK, NOPE + ROPE),
        span_latent,
        cache_latent,
        segments.reshape(CHIPS, CORES * TOK),
        prefix_len,
        w_uk,
        value_up_weight,
        w_out.T,
    )


def solution(mesh):
    placed = (
        P("seq", "head", None),
        P("seq", None),
        P("seq", None),
        P(),
        P(),
        P("head", None, None),
        P("head", None, None),
        P("head", "seq"),
    )
    return jax.shard_map(
        on_device, mesh=mesh, in_specs=placed, out_specs=P("seq", "head"), check_vma=False
    )
```

```python
import functools
import math

import jax
import jax.numpy as jnp
from jax import lax
from jax.experimental import pallas as pl
from jax.experimental.pallas import tpu as pltpu
from jax.sharding import PartitionSpec as P

MESH = pl.DeviceIdType.MESH
F32 = jnp.float32
BF16 = jnp.bfloat16

SIDE = 4
CHIPS = 16
CORES = 2
DEPTH = 8
TOK = 64
HEADS = 8
NOPE = 128
ROPE = 64
LAT = 512
VD = 128
COLS = 224
ROWS = HEADS * CORES * TOK
TILE = 512
KEYS = SIDE * TOK
LOW = -1e30
MASKED = -2e30

A, B, WHOLE = (0, 32), (32, 32), (0, 64)
Q = [(0, 16), (16, 16), (32, 16), (48, 16)]


def _by_neighbours():
    ev = [
        (0, 0, WHOLE, 0, 1),
        (0, 0, WHOLE, 0, 3),
        (0, 0, WHOLE, 1, 0),
        (0, 0, WHOLE, 3, 0),
        (0, 3, A, 0, 1),
        (0, 1, B, 0, 3),
        (3, 0, A, 1, 0),
        (1, 0, B, 3, 0),
    ]
    for dy in (3, 1, 2):
        ev += [(0, dy, A, 1, 0), (0, dy, A, 3, 0)]
    for dx in (3, 1, 2):
        ev += [(dx, 0, B, 0, 1), (dx, 0, B, 0, 3)]
    for dy in (3, 1, 2):
        ev += [(3, dy, Q[0], 1, 0), (1, dy, Q[1], 3, 0)]
    for dx in (3, 1, 2):
        ev += [(dx, 3, Q[2], 0, 1), (dx, 1, Q[3], 0, 3)]
    return ev


NEAR = _by_neighbours()
NEAR_1 = [(0, (4, 8, 9)), (1, (5, 10, 11)), (2, (6, 14, 15)), (3, (7, 16, 17))]
NEAR_2 = [
    (4, (12, 13)), (7, (18, 19)), (8, (20,)), (9, (21,)), (10, (22,)), (11, (23,)),
    (14, (26,)), (15, (27,)), (16, (28,)), (17, (29,)),
]
NEAR_3 = [(12, (24,)), (13, (25,)), (18, (30,)), (19, (31,))]


def _by_lines():
    ev = [(0, 0, WHOLE, 0, 1), (0, 0, WHOLE, 0, 3), (0, 0, WHOLE, 1, 0), (0, 0, WHOLE, 3, 0)]
    ev += [(0, 0, WHOLE, 0, 2), (0, 0, WHOLE, 2, 0)]
    ev += [(0, dy, A, sx, 0) for dy in (3, 1, 2) for sx in (1, 3, 2)]
    ev += [(dx, 0, B, 0, sy) for dx in (3, 1, 2) for sy in (1, 3, 2)]
    return ev


LINES = _by_lines()
LINES_1 = [
    (0, (6, 7, 8)), (1, (9, 10, 11)), (2, (15, 16, 17)), (3, (18, 19, 20)), (4, (12, 13, 14)), (5, (21, 22, 23)),
]


def kernel(
    q_hbm, span_hbm, cache_hbm, seg_hbm, pre_hbm, wuk_hbm, vup_hbm, wo_hbm, out_ref,
    q_ref, span_ref, cache_ref, seg_ref, pre_ref,
    kv, qs, qf, m_ref, l_ref, acc, bias, wuk, vup, wz, pp, pr, s1, r1, pha, s4, r4, r5,
    g1s, g1r, g2s, g2r, loc, sibs, sibr, wus, wur, wds, wdr, wps, wpr, s1s, s1r, s4s, s4r, s5s, s5r, known,
):
    s = lax.axis_index("seq")
    z = lax.axis_index("head")
    c = lax.rem(s, CORES)
    chip = s // CORES
    x = chip // SIDE
    y = lax.rem(chip, SIDE)

    def wrap(v, n):
        return lax.rem(v + n, n)

    def at(dx, dy):
        return wrap(x + dx, SIDE) * SIDE + wrap(y + dy, SIDE)

    def device(dx, dy):
        return (at(dx, dy) * CORES + c, z)

    sibling = (chip * CORES + 1 - c, z)
    up = (s, wrap(z + 1, DEPTH))
    down = (s, wrap(z + DEPTH - 1, DEPTH))

    copies = [
        pltpu.make_async_copy(src, dst, loc.at[i])
        for i, (src, dst) in enumerate(
            (
                (cache_hbm, cache_ref), (span_hbm, span_ref), (q_hbm, q_ref), (wuk_hbm, wuk),
                (seg_hbm, seg_ref), (pre_hbm, pre_ref), (vup_hbm, vup), (wo_hbm, wz.at[z, c]),
            )
        )
    ]
    for cp in copies:
        cp.start()

    barrier = pltpu.get_barrier_semaphore()
    near = [device(*d) for d in ((0, 1), (0, 3), (1, 0), (3, 0))] + [sibling, up, down]
    for dev in near:
        pl.semaphore_signal(barrier, inc=1, device_id=dev, device_id_type=MESH)

    copies[0].wait()
    copies[1].wait()
    kv[chip, :, 0:LAT] = cache_ref[:, 0:LAT]
    kv[chip, :, LAT : 2 * LAT] = span_ref[:, 0:LAT]
    kv[chip, :, 2 * LAT : 2 * LAT + 2 * ROPE] = jnp.concatenate(
        [cache_ref[:, LAT:], span_ref[:, LAT:]], axis=1
    )
    copies[2].wait()
    pl.semaphore_wait(barrier, len(near))

    def tell(n):
        for dev in (up, down):
            pl.semaphore_signal(known.at[n], inc=1, device_id=dev, device_id_type=MESH)

    def hear(n):
        pl.semaphore_wait(known.at[n], 2)

    tell(0)

    class Gather:
        def __init__(self, buf, send, recv, events, lanes):
            self.buf, self.send, self.recv, self.events, self.lanes = buf, send, recv, events, lanes

        def _copy(self, g, k, dx, dy, rows, sx, sy):
            ref = self.buf.at[at(dx, dy), pl.ds(*rows), pl.ds(*self.lanes[g])]
            n = g * len(self.events) + k
            return pltpu.make_async_remote_copy(
                src_ref=ref, dst_ref=ref, send_sem=self.send.at[n], recv_sem=self.recv.at[n],
                device_id=device(sx, sy), device_id_type=MESH,
            )

        def start(self, g, *ks):
            for k in ks:
                self._copy(g, k, *self.events[k]).start()

        def wait(self, g, *ks):
            for k in ks:
                dx, dy, rows, sx, sy = self.events[k]
                self._copy(g, k, (dx - sx) % 4, (dy - sy) % 4, rows, sx, sy).wait_recv()

        def follow(self, g, steps):
            for got, sends in steps:
                self.wait(g, got)
                self.start(g, *sends)

        def done(self):
            for g in range(len(self.lanes)):
                for k in range(len(self.events)):
                    self._copy(g, k, *self.events[k]).wait_send()

    def to_sibling(src, dst, k):
        return pltpu.make_async_remote_copy(
            src_ref=src, dst_ref=dst, send_sem=sibs.at[k], recv_sem=sibr.at[k],
            device_id=sibling, device_id_type=MESH,
        )

    keys = Gather(kv, g1s, g1r, NEAR, [(0, 2 * LAT + 2 * ROPE)])
    keys.start(0, 0, 1, 2, 3)
    q_swap = to_sibling(q_ref, qs, 0)
    q_swap.start()

    def around(way, i):
        half = i % 2 if way > 0 else (i + 1) % 2
        block = wrap(z - way * (i // 2) + DEPTH, DEPTH)
        ref = wz.at[block, c, pl.ds(half * (COLS // 2), COLS // 2)]
        send, recv = (wus, wur) if way > 0 else (wds, wdr)
        return pltpu.make_async_remote_copy(
            src_ref=ref, dst_ref=ref, send_sem=send.at[i], recv_sem=recv.at[i],
            device_id=up if way > 0 else down, device_id_type=MESH,
        )

    def around_landed(way, i):
        half = i % 2 if way > 0 else (i + 1) % 2
        block = wrap(z - way * (i // 2 + 1) + DEPTH, DEPTH)
        ref = wz.at[block, c, pl.ds(half * (COLS // 2), COLS // 2)]
        send, recv = (wus, wur) if way > 0 else (wds, wdr)
        pltpu.make_async_remote_copy(
            src_ref=ref, dst_ref=ref, send_sem=send.at[i], recv_sem=recv.at[i],
            device_id=up if way > 0 else down, device_id_type=MESH,
        ).wait_recv()

    def pass_block(d, core):
        ref = wz.at[wrap(z + d + DEPTH, DEPTH), core]
        return pltpu.make_async_remote_copy(
            src_ref=ref, dst_ref=ref, send_sem=wps.at[d % DEPTH], recv_sem=wpr.at[d % DEPTH],
            device_id=sibling, device_id_type=MESH,
        )

    def weights_step(i):
        for way in (1, -1):
            around_landed(way, i)
            if i < 3:
                around(way, i + 2).start()
        if i % 2 == 1:
            pass_block(i // 2 + 1, c).start()
            pass_block(-(i // 2 + 1), c).start()
        elif i == 6:
            pass_block(4, c).start()

    copies[7].wait()
    for i in range(2):
        around(1, i).start()
        around(-1, i).start()
    pass_block(0, c).start()

    m_ref[...] = jnp.full_like(m_ref, LOW)
    l_ref[...] = jnp.zeros_like(l_ref)
    acc[...] = jnp.zeros_like(acc)
    row = lax.broadcasted_iota(jnp.int32, (HEADS * TOK, HEADS * TOK), 0)
    col = lax.broadcasted_iota(jnp.int32, (HEADS * TOK, HEADS * TOK), 1)
    by_head = (col == lax.rem(row, TOK) * HEADS + row // TOK).astype(BF16)
    copies[3].wait()
    for src, core in ((q_ref, c), (qs, 1 - c)):
        if src is qs:
            q_swap.wait_recv()
        qp = jnp.dot(by_head, src[...], preferred_element_type=F32).astype(BF16)
        for h in range(HEADS):
            rows = pl.ds(pl.multiple_of(h * (CORES * TOK) + core * TOK, TOK), TOK)
            own = qp[h * TOK : (h + 1) * TOK]
            qf[rows, 0:LAT] = jnp.dot(own[:, 0:NOPE], wuk[h], preferred_element_type=F32).astype(BF16)
            qf[rows, LAT:] = jnp.concatenate([own[:, NOPE:], own[:, NOPE:]], axis=1)

    copies[4].wait()
    copies[5].wait()
    token = (chip * (CORES * TOK) + lax.broadcasted_iota(jnp.int32, (CORES * TOK, 1), 0)).astype(F32)
    segs = seg_ref[...]
    firsts = [
        jnp.sum(jnp.sum((segs < k).astype(F32), axis=1, keepdims=True), axis=0, keepdims=True)
        for k in (1, 2, 3)
    ]
    start_of = jnp.zeros_like(token)
    for first in firsts:
        start_of = jnp.maximum(start_of, jnp.where(token >= first, first, 0.0))
    prefix = pre_ref[0].astype(F32)
    cache_end = jnp.where(token < firsts[0], prefix - 1.0, -1.0)
    exponent = math.log2(math.e) / math.sqrt(NOPE + ROPE)

    def attend(*parts):
        latent, ropes, seen = [], [], []
        for kind, dx in parts:
            line = wrap(x + dx, SIDE)
            block = kv[pl.ds(line * SIDE, SIDE)].reshape(KEYS, 2 * LAT + 2 * ROPE)
            latent.append(block[:, kind * LAT : (kind + 1) * LAT])
            lane = lax.broadcasted_iota(jnp.int32, (KEYS, 2 * ROPE), 1)
            mine = lane < ROPE if kind == 0 else lane >= ROPE
            ropes.append(jnp.where(mine, block[:, 2 * LAT :], jnp.zeros((), BF16)))
            lane = lax.broadcasted_iota(jnp.int32, (1, KEYS), 1)
            pos = (
                line * (SIDE * CORES * TOK) + (lane // TOK) * (CORES * TOK) + c * TOK + lax.rem(lane, TOK)
            ).astype(F32)
            if kind == 0:
                seen.append(pos <= cache_end)
            else:
                seen.append(jnp.logical_and(pos >= start_of, pos <= token))
        values = jnp.concatenate(latent, axis=0)
        rows_k = jnp.concatenate([values, jnp.concatenate(ropes, axis=0)], axis=1)
        for i, ok in enumerate(seen):
            bias[:, i * KEYS : (i + 1) * KEYS] = jnp.where(ok, 0.0, MASKED)
        for i in range(ROWS // TILE):
            rows = slice(i * TILE, (i + 1) * TILE)
            sc = lax.dot_general(
                qf[rows, :], rows_k, (((1,), (1,)), ((), ())), preferred_element_type=F32
            )
            both = bias[...]
            sc = sc + jnp.concatenate([both] * (TILE // (CORES * TOK)), axis=0)
            m_old = m_ref[rows, :]
            m_new = jnp.maximum(m_old, jnp.max(sc, axis=1, keepdims=True))
            shrink = jnp.exp2((m_old - m_new) * exponent)
            p = jnp.exp2((sc - jnp.concatenate([m_new] * 4, axis=1)) * exponent)
            l_ref[rows, :] = l_ref[rows, :] * shrink + (
                (p[:, 0:128] + p[:, 128:256]) + (p[:, 256:384] + p[:, 384:512])
            )
            acc[rows, :] = acc[rows, :] * jnp.concatenate([shrink] * 4, axis=1) + jnp.dot(
                p.astype(BF16), values, preferred_element_type=F32
            )
            m_ref[rows, :] = m_new

    early = x < 2
    late = jnp.logical_not(early)

    keys.follow(0, NEAR_1)
    hear(0)
    tell(1)
    weights_step(0)
    keys.follow(0, NEAR_2)
    weights_step(1)
    keys.wait(0, 5)

    @pl.when(early)
    def _():
        attend((0, 0), (1, 0))

    hear(1)
    tell(2)
    keys.follow(0, NEAR_3)
    weights_step(2)
    keys.wait(0, 26, 27, 28, 29)

    @pl.when(early)
    def _():
        attend((0, 3), (0, 1))

    @pl.when(late)
    def _():
        attend((1, 0), (1, 3))

    keys.wait(0, 6, 20, 21, 22, 23, 24, 25, 30, 31)

    @pl.when(early)
    def _():
        attend((0, 2), (1, 3))

    @pl.when(late)
    def _():
        attend((1, 2), (1, 1))

    hear(2)

    copies[6].wait()
    half = lax.broadcasted_iota(jnp.int32, (CORES * TOK, 128), 1) < 64
    swaps = []
    for t in range(4):
        for h in (2 * t, 2 * t + 1):
            rows = slice(h * CORES * TOK, (h + 1) * CORES * TOK)
            total = jnp.sum(l_ref[rows, :], axis=1, keepdims=True)
            o = (acc[rows, :] / jnp.where(total > 0.0, total, 1.0)).astype(BF16)
            ph = jnp.dot(o, vup[h], preferred_element_type=F32)
            pp[:, h, :, 0:VD] = ph.reshape(CORES, TOK, VD)
            pp[:, h, :, VD:] = jnp.where(half, m_ref[rows, :], total).reshape(CORES, TOK, 128)
        swap = to_sibling(pp.at[1 - c, pl.ds(2 * t, 2)], pr.at[pl.ds(2 * t, 2)], 2 + t)
        swap.start()
        swaps.append(swap)
    def dealt(g, d):
        to = wrap(z + d, DEPTH)
        return pltpu.make_async_remote_copy(
            src_ref=s1.at[g, to], dst_ref=r1.at[g, z], send_sem=s1s.at[g * DEPTH + d], recv_sem=s1r.at[g * DEPTH + z],
            device_id=(s, to), device_id_type=MESH,
        )

    def landed(src, dst, sem):
        pltpu.make_async_remote_copy(
            src_ref=src, dst_ref=dst, send_sem=s1s.at[0], recv_sem=sem, device_id=up, device_id_type=MESH
        ).wait_recv()

    far_first = (4, 3, 5, 2, 6, 1, 7)
    wide = HEADS * VD // 2
    for g in range(2):
        merged = []
        for t in (2 * g, 2 * g + 1):
            swaps[t].wait_recv()
            for h in (2 * t, 2 * t + 1):
                own, other = pp[c, h], pr[h]
                m0, m1 = own[:, VD : VD + 1], other[:, VD : VD + 1]
                l0, l1 = own[:, VD + 64 : VD + 65], other[:, VD + 64 : VD + 65]
                top = jnp.maximum(m0, m1)
                w0 = l0 * jnp.exp2((m0 - top) * exponent)
                w1 = l1 * jnp.exp2((m1 - top) * exponent)
                norm = w0 + w1
                merged.append(own[:, 0:VD] * (w0 / norm) + other[:, 0:VD] * (w1 / norm))
        left = jnp.concatenate(merged[:2], axis=1)
        right = jnp.concatenate(merged[2:], axis=1)
        for p in range(DEPTH):
            rows = slice(8 * p, 8 * p + 8)
            s1[g, p] = jnp.concatenate([left[rows], right[rows]], axis=0).astype(BF16)
        for d in far_first:
            dealt(g, d).start()
        r1[g, z] = s1[g, z]

    heads = Gather(pha, g2s, g2r, LINES, [(0, wide), (wide, wide)])
    for g in range(2):
        for d in reversed(far_first):
            plane = wrap(z + d, DEPTH)
            landed(s1.at[0, 0], r1.at[g, plane], s1r.at[g * DEPTH + plane])
        blocks = []
        for p in range(DEPTH):
            rows = r1[g, p].astype(F32)
            blocks.append(jnp.concatenate([rows[0:8], rows[8:16]], axis=1))
        pha[chip, :, g * wide : (g + 1) * wide] = jnp.concatenate(blocks, axis=0).astype(BF16)
        heads.start(g, 4, 5, 0, 1, 2, 3)
    weights_step(3)
    weights_step(4)
    for i in (5, 6):
        around(1, i).start()
        around(-1, i).start()
    for g in range(2):
        heads.follow(g, LINES_1)
    keys.done()
    q_swap.wait_send()
    for t in range(4):
        swaps[t].wait_send()
    for d in far_first:
        dealt(0, d).wait_send()
        dealt(1, d).wait_send()
    weights_step(5)
    weights_step(6)
    for d in range(DEPTH):
        pass_block(d, 1 - c).wait_recv()

    even = lax.rem(lax.broadcasted_iota(jnp.int32, (COLS, CHIPS * 16), 1), 16) < 8
    sums = [[None, None], [None, None]]
    for g in range(2):
        heads.wait(g, *range(6, 24))
        lanes = slice(g * wide, (g + 1) * wide)
        for i in range(CORES):
            for parity in range(2):
                total = sums[i][parity]
                for p in range(DEPTH // 2):
                    rows = pha[:, 16 * p : 16 * p + 16, lanes].reshape(CHIPS * 16, wide)
                    v = lax.dot_general(
                        wz[2 * p + parity, i, :, lanes], rows, (((1,), (1,)), ((), ())),
                        preferred_element_type=F32,
                    )
                    total = v if total is None else total + v
                sums[i][parity] = total
    products = [jnp.where(even, *pair).T for pair in sums]
    for g in range(CHIPS):
        s4[g] = jnp.concatenate(
            [v[16 * g : 16 * g + 8] + v[16 * g + 8 : 16 * g + 16] for v in products], axis=0
        ).astype(BF16)

    others = [(dx, dy) for dx in (2, 1, 3, 0) for dy in (2, 1, 3, 0)][:-1]

    def over(dx, dy):
        return pltpu.make_async_remote_copy(
            src_ref=s4.at[at(dx, dy)], dst_ref=r4.at[chip], send_sem=s4s.at[dx * SIDE + dy], recv_sem=s4r.at[chip],
            device_id=device(dx, dy), device_id_type=MESH,
        )

    def along(d):
        plane = wrap(z + d, DEPTH)
        return pltpu.make_async_remote_copy(
            src_ref=r4.at[pl.ds(2 * plane, 2)], dst_ref=r5.at[z], send_sem=s5s.at[d], recv_sem=s5r.at[z],
            device_id=(s, plane), device_id_type=MESH,
        )

    for dx, dy in others:
        over(dx, dy).start()
    r4[chip] = s4[chip]
    heads.done()
    for i in range(7):
        around(1, i).wait_send()
        around(-1, i).wait_send()
    for d in range(DEPTH):
        pass_block(d, c).wait_send()
    for dx, dy in reversed(others):
        landed(s4.at[0], r4.at[at(dx, dy)], s4r.at[at(dx, dy)])
    for d in far_first:
        along(d).start()
    r5[z] = r4[pl.ds(2 * z, 2)]
    for dx, dy in others:
        over(dx, dy).wait_send()
    for d in reversed(far_first):
        plane = wrap(z + d, DEPTH)
        landed(r4.at[pl.ds(0, 2)], r5.at[plane], s5r.at[plane])
    columns = []
    for a in range(2):
        for i in range(CORES):
            columns.append(
                jnp.concatenate([r5[p, a].astype(F32)[8 * i : 8 * i + 8] for p in range(DEPTH)], axis=0)
            )
    out_ref[...] = jnp.concatenate(columns, axis=1).astype(BF16)

    for d in far_first:
        along(d).wait_send()


def on_device(queries, span_latent, cache_latent, segments, prefix_len, w_uk, value_up_weight, w_out):
    hbm = pl.BlockSpec(memory_space=pltpu.HBM)
    dma = pltpu.SemaphoreType.DMA
    return pl.pallas_call(
        kernel,
        out_shape=jax.ShapeDtypeStruct((TOK, CORES * 2 * COLS), BF16),
        in_specs=[hbm] * 8,
        out_specs=pl.BlockSpec(memory_space=pltpu.VMEM),
        scratch_shapes=[
            pltpu.VMEM((HEADS * TOK, NOPE + ROPE), BF16),
            pltpu.VMEM((TOK, LAT + ROPE), BF16),
            pltpu.VMEM((TOK, LAT + ROPE), BF16),
            pltpu.VMEM((CHIPS, CORES * TOK), jnp.int32),
            pltpu.SMEM((1,), jnp.int32),
            pltpu.VMEM((CHIPS, TOK, 2 * LAT + 2 * ROPE), BF16),
            pltpu.VMEM((HEADS * TOK, NOPE + ROPE), BF16),
            pltpu.VMEM((ROWS, LAT + 2 * ROPE), BF16),
            pltpu.VMEM((ROWS, 128), F32),
            pltpu.VMEM((ROWS, 128), F32),
            pltpu.VMEM((ROWS, LAT), F32),
            pltpu.VMEM((CORES * TOK, 2 * KEYS), F32),
            pltpu.VMEM((HEADS, NOPE, LAT), BF16),
            pltpu.VMEM((HEADS, LAT, VD), BF16),
            pltpu.VMEM((DEPTH, CORES, COLS, HEADS * VD), BF16),
            pltpu.VMEM((CORES, HEADS, TOK, 2 * VD), F32),
            pltpu.VMEM((HEADS, TOK, 2 * VD), F32),
            pltpu.VMEM((2, DEPTH, 16, HEADS * VD // 4), BF16),
            pltpu.VMEM((2, DEPTH, 16, HEADS * VD // 4), BF16),
            pltpu.VMEM((CHIPS, TOK, HEADS * VD), BF16),
            pltpu.VMEM((CHIPS, 16, COLS), BF16),
            pltpu.VMEM((CHIPS, 16, COLS), BF16),
            pltpu.VMEM((DEPTH, 2, 16, COLS), BF16),
            dma((32,)), dma((32,)), dma((48,)), dma((48,)),
            dma((8,)), dma((6,)), dma((6,)), dma((7,)), dma((7,)), dma((7,)), dma((7,)), dma((8,)), dma((8,)),
            dma((16,)), dma((16,)), dma((16,)), dma((16,)), dma((8,)), dma((8,)),
            pltpu.SemaphoreType.REGULAR((3,)),
        ],
        compiler_params=pltpu.CompilerParams(
            collective_id=0, has_side_effects=True, vmem_limit_bytes=56 * 1024 * 1024
        ),
        name="prefill",
    )(
        queries.reshape(HEADS * TOK, NOPE + ROPE),
        span_latent,
        cache_latent,
        segments.reshape(CHIPS, CORES * TOK),
        prefix_len,
        w_uk,
        value_up_weight,
        w_out.T,
    )


def solution(mesh):
    placed = (
        P("seq", "head", None),
        P("seq", None),
        P("seq", None),
        P(),
        P(),
        P("head", None, None),
        P("head", None, None),
        P("head", "seq"),
    )
    return jax.shard_map(
        on_device, mesh=mesh, in_specs=placed, out_specs=P("seq", "head"), check_vma=False
    )
```

```python
import functools
import math

import jax
import jax.numpy as jnp
from jax import lax
from jax.experimental import pallas as pl
from jax.experimental.pallas import tpu as pltpu
from jax.sharding import PartitionSpec as P

MESH = pl.DeviceIdType.MESH
F32 = jnp.float32
BF16 = jnp.bfloat16

SIDE = 4
CHIPS = 16
CORES = 2
DEPTH = 8
TOK = 64
HEADS = 8
NOPE = 128
ROPE = 64
LAT = 512
VD = 128
COLS = 224
ROWS = HEADS * CORES * TOK
TILE = 512
KEYS = SIDE * TOK
LOW = -1e30
MASKED = -2e30

A, B, WHOLE = (0, 32), (32, 32), (0, 64)
Q = [(0, 16), (16, 16), (32, 16), (48, 16)]


def _by_neighbours():
    ev = [
        (0, 0, WHOLE, 0, 1),
        (0, 0, WHOLE, 0, 3),
        (0, 0, WHOLE, 1, 0),
        (0, 0, WHOLE, 3, 0),
        (0, 3, A, 0, 1),
        (0, 1, B, 0, 3),
        (3, 0, A, 1, 0),
        (1, 0, B, 3, 0),
    ]
    for dy in (3, 1, 2):
        ev += [(0, dy, A, 1, 0), (0, dy, A, 3, 0)]
    for dx in (3, 1, 2):
        ev += [(dx, 0, B, 0, 1), (dx, 0, B, 0, 3)]
    for dy in (3, 1, 2):
        ev += [(3, dy, Q[0], 1, 0), (1, dy, Q[1], 3, 0)]
    for dx in (3, 1, 2):
        ev += [(dx, 3, Q[2], 0, 1), (dx, 1, Q[3], 0, 3)]
    return ev


NEAR = _by_neighbours()
NEAR_1 = [(0, (4, 8, 9)), (1, (5, 10, 11)), (2, (6, 14, 15)), (3, (7, 16, 17))]
NEAR_2 = [
    (4, (12, 13)), (7, (18, 19)), (8, (20,)), (9, (21,)), (10, (22,)), (11, (23,)),
    (14, (26,)), (15, (27,)), (16, (28,)), (17, (29,)),
]
NEAR_3 = [(12, (24,)), (13, (25,)), (18, (30,)), (19, (31,))]


def _by_lines():
    ev = [(0, 0, WHOLE, 0, 1), (0, 0, WHOLE, 0, 3), (0, 0, WHOLE, 1, 0), (0, 0, WHOLE, 3, 0)]
    ev += [(0, 0, WHOLE, 0, 2), (0, 0, WHOLE, 2, 0)]
    ev += [(0, dy, A, sx, 0) for dy in (3, 1, 2) for sx in (1, 3, 2)]
    ev += [(dx, 0, B, 0, sy) for dx in (3, 1, 2) for sy in (1, 3, 2)]
    return ev


LINES = _by_lines()
LINES_1 = [
    (0, (6, 7, 8)), (1, (9, 10, 11)), (2, (15, 16, 17)), (3, (18, 19, 20)), (4, (12, 13, 14)), (5, (21, 22, 23)),
]


def kernel(
    q_hbm, span_hbm, cache_hbm, seg_hbm, pre_hbm, wuk_hbm, vup_hbm, wo_hbm, out_ref,
    q_ref, span_ref, cache_ref, seg_ref, pre_ref,
    kv, qs, qf, m_ref, l_ref, acc, bias, wuk, vup, wz, pp, pr, s1, r1, pha, s4, r4, r5,
    g1s, g1r, g2s, g2r, loc, sibs, sibr, wus, wur, wds, wdr, wps, wpr, s1s, s1r, s4s, s4r, s5s, s5r, known,
):
    s = lax.axis_index("seq")
    z = lax.axis_index("head")
    c = lax.rem(s, CORES)
    chip = s // CORES
    x = chip // SIDE
    y = lax.rem(chip, SIDE)

    def wrap(v, n):
        return lax.rem(v + n, n)

    def at(dx, dy):
        return wrap(x + dx, SIDE) * SIDE + wrap(y + dy, SIDE)

    def device(dx, dy):
        return (at(dx, dy) * CORES + c, z)

    sibling = (chip * CORES + 1 - c, z)
    up = (s, wrap(z + 1, DEPTH))
    down = (s, wrap(z + DEPTH - 1, DEPTH))

    copies = [
        pltpu.make_async_copy(src, dst, loc.at[i])
        for i, (src, dst) in enumerate(
            (
                (cache_hbm, cache_ref), (span_hbm, span_ref), (q_hbm, q_ref), (wuk_hbm, wuk),
                (seg_hbm, seg_ref), (pre_hbm, pre_ref), (vup_hbm, vup), (wo_hbm, wz.at[z, c]),
            )
        )
    ]
    for cp in copies:
        cp.start()

    barrier = pltpu.get_barrier_semaphore()
    near = [device(*d) for d in ((0, 1), (0, 3), (1, 0), (3, 0))] + [sibling, up, down]
    for dev in near:
        pl.semaphore_signal(barrier, inc=1, device_id=dev, device_id_type=MESH)

    copies[0].wait()
    copies[1].wait()
    kv[chip, :, 0:LAT] = cache_ref[:, 0:LAT]
    kv[chip, :, LAT : 2 * LAT] = span_ref[:, 0:LAT]
    kv[chip, :, 2 * LAT : 2 * LAT + 2 * ROPE] = jnp.concatenate(
        [cache_ref[:, LAT:], span_ref[:, LAT:]], axis=1
    )
    copies[2].wait()
    pl.semaphore_wait(barrier, len(near))

    def tell(n):
        for dev in (up, down):
            pl.semaphore_signal(known.at[n], inc=1, device_id=dev, device_id_type=MESH)

    def hear(n):
        pl.semaphore_wait(known.at[n], 2)

    tell(0)

    class Gather:
        def __init__(self, buf, send, recv, events, lanes):
            self.buf, self.send, self.recv, self.events, self.lanes = buf, send, recv, events, lanes

        def _copy(self, g, k, dx, dy, rows, sx, sy):
            ref = self.buf.at[at(dx, dy), pl.ds(*rows), pl.ds(*self.lanes[g])]
            n = g * len(self.events) + k
            return pltpu.make_async_remote_copy(
                src_ref=ref, dst_ref=ref, send_sem=self.send.at[n], recv_sem=self.recv.at[n],
                device_id=device(sx, sy), device_id_type=MESH,
            )

        def start(self, g, *ks):
            for k in ks:
                self._copy(g, k, *self.events[k]).start()

        def wait(self, g, *ks):
            for k in ks:
                dx, dy, rows, sx, sy = self.events[k]
                self._copy(g, k, (dx - sx) % 4, (dy - sy) % 4, rows, sx, sy).wait_recv()

        def follow(self, g, steps):
            for got, sends in steps:
                self.wait(g, got)
                self.start(g, *sends)

        def done(self):
            for g in range(len(self.lanes)):
                for k in range(len(self.events)):
                    self._copy(g, k, *self.events[k]).wait_send()

    def to_sibling(src, dst, k):
        return pltpu.make_async_remote_copy(
            src_ref=src, dst_ref=dst, send_sem=sibs.at[k], recv_sem=sibr.at[k],
            device_id=sibling, device_id_type=MESH,
        )

    keys = Gather(kv, g1s, g1r, NEAR, [(0, 2 * LAT + 2 * ROPE)])
    keys.start(0, 0, 1, 2, 3)
    q_swap = to_sibling(q_ref, qs, 0)
    q_swap.start()

    def around(way, i):
        half = i % 2 if way > 0 else (i + 1) % 2
        block = wrap(z - way * (i // 2) + DEPTH, DEPTH)
        ref = wz.at[block, c, pl.ds(half * (COLS // 2), COLS // 2)]
        send, recv = (wus, wur) if way > 0 else (wds, wdr)
        return pltpu.make_async_remote_copy(
            src_ref=ref, dst_ref=ref, send_sem=send.at[i], recv_sem=recv.at[i],
            device_id=up if way > 0 else down, device_id_type=MESH,
        )

    def around_landed(way, i):
        half = i % 2 if way > 0 else (i + 1) % 2
        block = wrap(z - way * (i // 2 + 1) + DEPTH, DEPTH)
        ref = wz.at[block, c, pl.ds(half * (COLS // 2), COLS // 2)]
        send, recv = (wus, wur) if way > 0 else (wds, wdr)
        pltpu.make_async_remote_copy(
            src_ref=ref, dst_ref=ref, send_sem=send.at[i], recv_sem=recv.at[i],
            device_id=up if way > 0 else down, device_id_type=MESH,
        ).wait_recv()

    def pass_block(d, core):
        ref = wz.at[wrap(z + d + DEPTH, DEPTH), core]
        return pltpu.make_async_remote_copy(
            src_ref=ref, dst_ref=ref, send_sem=wps.at[d % DEPTH], recv_sem=wpr.at[d % DEPTH],
            device_id=sibling, device_id_type=MESH,
        )

    def weights_step(i):
        for way in (1, -1):
            around_landed(way, i)
            if i < 3:
                around(way, i + 2).start()
        if i % 2 == 1:
            pass_block(i // 2 + 1, c).start()
            pass_block(-(i // 2 + 1), c).start()
        elif i == 6:
            pass_block(4, c).start()

    copies[7].wait()
    for i in range(2):
        around(1, i).start()
        around(-1, i).start()
    pass_block(0, c).start()

    m_ref[...] = jnp.full_like(m_ref, LOW)
    l_ref[...] = jnp.zeros_like(l_ref)
    acc[...] = jnp.zeros_like(acc)
    row = lax.broadcasted_iota(jnp.int32, (HEADS * TOK, HEADS * TOK), 0)
    col = lax.broadcasted_iota(jnp.int32, (HEADS * TOK, HEADS * TOK), 1)
    by_head = (col == lax.rem(row, TOK) * HEADS + row // TOK).astype(BF16)
    copies[3].wait()
    for src, core in ((q_ref, c), (qs, 1 - c)):
        if src is qs:
            q_swap.wait_recv()
        qp = jnp.dot(by_head, src[...], preferred_element_type=F32).astype(BF16)
        for h in range(HEADS):
            rows = pl.ds(pl.multiple_of(h * (CORES * TOK) + core * TOK, TOK), TOK)
            own = qp[h * TOK : (h + 1) * TOK]
            qf[rows, 0:LAT] = jnp.dot(own[:, 0:NOPE], wuk[h], preferred_element_type=F32).astype(BF16)
            qf[rows, LAT:] = jnp.concatenate([own[:, NOPE:], own[:, NOPE:]], axis=1)

    copies[4].wait()
    copies[5].wait()
    token = (chip * (CORES * TOK) + lax.broadcasted_iota(jnp.int32, (CORES * TOK, 1), 0)).astype(F32)
    segs = seg_ref[...]
    firsts = [
        jnp.sum(jnp.sum((segs < k).astype(F32), axis=1, keepdims=True), axis=0, keepdims=True)
        for k in (1, 2, 3)
    ]
    start_of = jnp.zeros_like(token)
    for first in firsts:
        start_of = jnp.maximum(start_of, jnp.where(token >= first, first, 0.0))
    prefix = pre_ref[0].astype(F32)
    cache_end = jnp.where(token < firsts[0], prefix - 1.0, -1.0)
    exponent = math.log2(math.e) / math.sqrt(NOPE + ROPE)

    def attend(*parts):
        latent, ropes, seen = [], [], []
        for kind, dx in parts:
            line = wrap(x + dx, SIDE)
            block = kv[pl.ds(line * SIDE, SIDE)].reshape(KEYS, 2 * LAT + 2 * ROPE)
            latent.append(block[:, kind * LAT : (kind + 1) * LAT])
            lane = lax.broadcasted_iota(jnp.int32, (KEYS, 2 * ROPE), 1)
            mine = lane < ROPE if kind == 0 else lane >= ROPE
            ropes.append(jnp.where(mine, block[:, 2 * LAT :], jnp.zeros((), BF16)))
            lane = lax.broadcasted_iota(jnp.int32, (1, KEYS), 1)
            pos = (
                line * (SIDE * CORES * TOK) + (lane // TOK) * (CORES * TOK) + c * TOK + lax.rem(lane, TOK)
            ).astype(F32)
            if kind == 0:
                seen.append(pos <= cache_end)
            else:
                seen.append(jnp.logical_and(pos >= start_of, pos <= token))
        values = jnp.concatenate(latent, axis=0)
        rows_k = jnp.concatenate([values, jnp.concatenate(ropes, axis=0)], axis=1)
        for i, ok in enumerate(seen):
            bias[:, i * KEYS : (i + 1) * KEYS] = jnp.where(ok, 0.0, MASKED)
        for i in range(ROWS // TILE):
            rows = slice(i * TILE, (i + 1) * TILE)
            sc = lax.dot_general(
                qf[rows, :], rows_k, (((1,), (1,)), ((), ())), preferred_element_type=F32
            )
            both = bias[...]
            sc = sc + jnp.concatenate([both] * (TILE // (CORES * TOK)), axis=0)
            m_old = m_ref[rows, :]
            m_new = jnp.maximum(m_old, jnp.max(sc, axis=1, keepdims=True))
            shrink = jnp.exp2((m_old - m_new) * exponent)
            p = jnp.exp2((sc - jnp.concatenate([m_new] * 4, axis=1)) * exponent)
            l_ref[rows, :] = l_ref[rows, :] * shrink + (
                (p[:, 0:128] + p[:, 128:256]) + (p[:, 256:384] + p[:, 384:512])
            )
            acc[rows, :] = acc[rows, :] * jnp.concatenate([shrink] * 4, axis=1) + jnp.dot(
                p.astype(BF16), values, preferred_element_type=F32
            )
            m_ref[rows, :] = m_new

    early = x < 2
    late = jnp.logical_not(early)

    keys.follow(0, NEAR_1)
    hear(0)
    tell(1)
    weights_step(0)
    keys.follow(0, NEAR_2)
    weights_step(1)
    keys.wait(0, 5)

    @pl.when(early)
    def _():
        attend((0, 0), (1, 0))

    hear(1)
    tell(2)
    keys.follow(0, NEAR_3)
    weights_step(2)
    keys.wait(0, 26, 27, 28, 29)

    @pl.when(early)
    def _():
        attend((0, 3), (0, 1))

    @pl.when(late)
    def _():
        attend((1, 0), (1, 3))

    keys.wait(0, 6, 20, 21, 22, 23, 24, 25, 30, 31)

    @pl.when(early)
    def _():
        attend((0, 2), (1, 3))

    @pl.when(late)
    def _():
        attend((1, 2), (1, 1))

    hear(2)

    copies[6].wait()
    half = lax.broadcasted_iota(jnp.int32, (CORES * TOK, 128), 1) < 64
    swaps = []
    for t in range(4):
        for h in (2 * t, 2 * t + 1):
            rows = slice(h * CORES * TOK, (h + 1) * CORES * TOK)
            total = jnp.sum(l_ref[rows, :], axis=1, keepdims=True)
            o = (acc[rows, :] * (1.0 / jnp.where(total > 0.0, total, 1.0))).astype(BF16)
            ph = jnp.dot(o, vup[h], preferred_element_type=F32)
            pp[:, h, :, 0:VD] = ph.reshape(CORES, TOK, VD)
            pp[:, h, :, VD:] = jnp.where(half, m_ref[rows, :], total).reshape(CORES, TOK, 128)
        swap = to_sibling(pp.at[1 - c, pl.ds(2 * t, 2)], pr.at[pl.ds(2 * t, 2)], 2 + t)
        swap.start()
        swaps.append(swap)
    def dealt(g, d):
        to = wrap(z + d, DEPTH)
        return pltpu.make_async_remote_copy(
            src_ref=s1.at[g, to], dst_ref=r1.at[g, z], send_sem=s1s.at[g * DEPTH + d], recv_sem=s1r.at[g * DEPTH + z],
            device_id=(s, to), device_id_type=MESH,
        )

    def landed(src, dst, sem):
        pltpu.make_async_remote_copy(
            src_ref=src, dst_ref=dst, send_sem=s1s.at[0], recv_sem=sem, device_id=up, device_id_type=MESH
        ).wait_recv()

    far_first = (4, 3, 5, 2, 6, 1, 7)
    wide = HEADS * VD // 2
    for g in range(2):
        merged = []
        for t in (2 * g, 2 * g + 1):
            swaps[t].wait_recv()
            for h in (2 * t, 2 * t + 1):
                own, other = pp[c, h], pr[h]
                m0, m1 = own[:, VD : VD + 1], other[:, VD : VD + 1]
                l0, l1 = own[:, VD + 64 : VD + 65], other[:, VD + 64 : VD + 65]
                top = jnp.maximum(m0, m1)
                w0 = l0 * jnp.exp2((m0 - top) * exponent)
                w1 = l1 * jnp.exp2((m1 - top) * exponent)
                norm = w0 + w1
                merged.append(own[:, 0:VD] * (w0 / norm) + other[:, 0:VD] * (w1 / norm))
        left = jnp.concatenate(merged[:2], axis=1)
        right = jnp.concatenate(merged[2:], axis=1)
        for p in range(DEPTH):
            rows = slice(8 * p, 8 * p + 8)
            s1[g, p] = jnp.concatenate([left[rows], right[rows]], axis=0).astype(BF16)
        for d in far_first:
            dealt(g, d).start()
        r1[g, z] = s1[g, z]

    heads = Gather(pha, g2s, g2r, LINES, [(0, wide), (wide, wide)])
    for g in range(2):
        for d in reversed(far_first):
            plane = wrap(z + d, DEPTH)
            landed(s1.at[0, 0], r1.at[g, plane], s1r.at[g * DEPTH + plane])
        blocks = []
        for p in range(DEPTH):
            rows = r1[g, p].astype(F32)
            blocks.append(jnp.concatenate([rows[0:8], rows[8:16]], axis=1))
        pha[chip, :, g * wide : (g + 1) * wide] = jnp.concatenate(blocks, axis=0).astype(BF16)
        heads.start(g, 4, 5, 0, 1, 2, 3)
    weights_step(3)
    weights_step(4)
    for i in (5, 6):
        around(1, i).start()
        around(-1, i).start()
    for g in range(2):
        heads.follow(g, LINES_1)
    keys.done()
    q_swap.wait_send()
    for t in range(4):
        swaps[t].wait_send()
    for d in far_first:
        dealt(0, d).wait_send()
        dealt(1, d).wait_send()
    weights_step(5)
    weights_step(6)
    for d in range(DEPTH):
        pass_block(d, 1 - c).wait_recv()

    even = lax.rem(lax.broadcasted_iota(jnp.int32, (COLS, CHIPS * 16), 1), 16) < 8
    sums = [[None, None], [None, None]]
    for g in range(2):
        heads.wait(g, *range(6, 24))
        lanes = slice(g * wide, (g + 1) * wide)
        for i in range(CORES):
            for parity in range(2):
                total = sums[i][parity]
                for p in range(DEPTH // 2):
                    rows = pha[:, 16 * p : 16 * p + 16, lanes].reshape(CHIPS * 16, wide)
                    v = lax.dot_general(
                        wz[2 * p + parity, i, :, lanes], rows, (((1,), (1,)), ((), ())),
                        preferred_element_type=F32,
                    )
                    total = v if total is None else total + v
                sums[i][parity] = total
    products = [jnp.where(even, *pair).T for pair in sums]
    for g in range(CHIPS):
        s4[g] = jnp.concatenate(
            [v[16 * g : 16 * g + 8] + v[16 * g + 8 : 16 * g + 16] for v in products], axis=0
        ).astype(BF16)

    others = [(dx, dy) for dx in (2, 1, 3, 0) for dy in (2, 1, 3, 0)][:-1]

    def over(dx, dy):
        return pltpu.make_async_remote_copy(
            src_ref=s4.at[at(dx, dy)], dst_ref=r4.at[chip], send_sem=s4s.at[dx * SIDE + dy], recv_sem=s4r.at[chip],
            device_id=device(dx, dy), device_id_type=MESH,
        )

    def along(d):
        plane = wrap(z + d, DEPTH)
        return pltpu.make_async_remote_copy(
            src_ref=r4.at[pl.ds(2 * plane, 2)], dst_ref=r5.at[z], send_sem=s5s.at[d], recv_sem=s5r.at[z],
            device_id=(s, plane), device_id_type=MESH,
        )

    for dx, dy in others:
        over(dx, dy).start()
    r4[chip] = s4[chip]
    heads.done()
    for i in range(7):
        around(1, i).wait_send()
        around(-1, i).wait_send()
    for d in range(DEPTH):
        pass_block(d, c).wait_send()
    for dx, dy in reversed(others):
        landed(s4.at[0], r4.at[at(dx, dy)], s4r.at[at(dx, dy)])
    for d in far_first:
        along(d).start()
    r5[z] = r4[pl.ds(2 * z, 2)]
    for dx, dy in others:
        over(dx, dy).wait_send()
    for d in reversed(far_first):
        plane = wrap(z + d, DEPTH)
        landed(r4.at[pl.ds(0, 2)], r5.at[plane], s5r.at[plane])
    columns = []
    for a in range(2):
        for i in range(CORES):
            columns.append(
                jnp.concatenate([r5[p, a].astype(F32)[8 * i : 8 * i + 8] for p in range(DEPTH)], axis=0)
            )
    out_ref[...] = jnp.concatenate(columns, axis=1).astype(BF16)

    for d in far_first:
        along(d).wait_send()


def on_device(queries, span_latent, cache_latent, segments, prefix_len, w_uk, value_up_weight, w_out):
    hbm = pl.BlockSpec(memory_space=pltpu.HBM)
    dma = pltpu.SemaphoreType.DMA
    return pl.pallas_call(
        kernel,
        out_shape=jax.ShapeDtypeStruct((TOK, CORES * 2 * COLS), BF16),
        in_specs=[hbm] * 8,
        out_specs=pl.BlockSpec(memory_space=pltpu.VMEM),
        scratch_shapes=[
            pltpu.VMEM((HEADS * TOK, NOPE + ROPE), BF16),
            pltpu.VMEM((TOK, LAT + ROPE), BF16),
            pltpu.VMEM((TOK, LAT + ROPE), BF16),
            pltpu.VMEM((CHIPS, CORES * TOK), jnp.int32),
            pltpu.SMEM((1,), jnp.int32),
            pltpu.VMEM((CHIPS, TOK, 2 * LAT + 2 * ROPE), BF16),
            pltpu.VMEM((HEADS * TOK, NOPE + ROPE), BF16),
            pltpu.VMEM((ROWS, LAT + 2 * ROPE), BF16),
            pltpu.VMEM((ROWS, 128), F32),
            pltpu.VMEM((ROWS, 128), F32),
            pltpu.VMEM((ROWS, LAT), F32),
            pltpu.VMEM((CORES * TOK, 2 * KEYS), F32),
            pltpu.VMEM((HEADS, NOPE, LAT), BF16),
            pltpu.VMEM((HEADS, LAT, VD), BF16),
            pltpu.VMEM((DEPTH, CORES, COLS, HEADS * VD), BF16),
            pltpu.VMEM((CORES, HEADS, TOK, 2 * VD), F32),
            pltpu.VMEM((HEADS, TOK, 2 * VD), F32),
            pltpu.VMEM((2, DEPTH, 16, HEADS * VD // 4), BF16),
            pltpu.VMEM((2, DEPTH, 16, HEADS * VD // 4), BF16),
            pltpu.VMEM((CHIPS, TOK, HEADS * VD), BF16),
            pltpu.VMEM((CHIPS, 16, COLS), BF16),
            pltpu.VMEM((CHIPS, 16, COLS), BF16),
            pltpu.VMEM((DEPTH, 2, 16, COLS), BF16),
            dma((32,)), dma((32,)), dma((48,)), dma((48,)),
            dma((8,)), dma((6,)), dma((6,)), dma((7,)), dma((7,)), dma((7,)), dma((7,)), dma((8,)), dma((8,)),
            dma((16,)), dma((16,)), dma((16,)), dma((16,)), dma((8,)), dma((8,)),
            pltpu.SemaphoreType.REGULAR((3,)),
        ],
        compiler_params=pltpu.CompilerParams(
            collective_id=0, has_side_effects=True, vmem_limit_bytes=56 * 1024 * 1024
        ),
        name="prefill",
    )(
        queries.reshape(HEADS * TOK, NOPE + ROPE),
        span_latent,
        cache_latent,
        segments.reshape(CHIPS, CORES * TOK),
        prefix_len,
        w_uk,
        value_up_weight,
        w_out.T,
    )


def solution(mesh):
    placed = (
        P("seq", "head", None),
        P("seq", None),
        P("seq", None),
        P(),
        P(),
        P("head", None, None),
        P("head", None, None),
        P("head", "seq"),
    )
    return jax.shard_map(
        on_device, mesh=mesh, in_specs=placed, out_specs=P("seq", "head"), check_vma=False
    )
```
